32 devices in a mesh: gz: 8 (over z, x), vert: 4 (over y, core).
Axes of the slice: x: 2, y: 2, z: 4, core: 2. Of those that a mesh axis runs over, the one named last changes fastest.
Arguments:
- estimate: float32 [128, 128, 256], P('gz'), may hold values from 0.5 to 2
- raw_views: bfloat16 [12, 1024, 16, 256], P('vert', 'gz'), may hold values from 0.3 to 3, as said below
- block_dest: int32 [12, 1024], P('vert', 'gz'), may hold values from 0 to 1023, as said below
- lateral_psf: float32 [12, 2, 17], P('vert'), may hold values from 0.05 to 1
- axial_psf: float32 [12, 17], P('vert'), may hold values from 0.05 to 1
Outputs:
- restored: float32 [128, 128, 256], P('gz')
The draws below stay inside these ranges and needn't reach their ends.
Inputs may be any that keep to these rules, and one draw needn't show every extreme that they name: `block_dest`: for each view the values are a permutation of all block places; a value p lies in slab p // 128. The blocks of one view held by one index of gz go to their slabs in groups of exactly 16 blocks, except one slab that receives exactly 32; every slab receives 128 blocks of each view. `raw_views`: positive intensities.
All inputs are finite; a program needn't handle non-finite values.
Results may differ from the reference program's by a relative error of at most 0.00044.
Values may be sent and summed in bfloat16 or wider, within the bound.
A program may use at most 128 MiB of HBM per device.

```python
import math
import jax
import jax.numpy as jnp
from jax import lax

VIEWS = 12
WX = 128
WY = 256
BAND = 16
ITERS = 2
NZ = 128
BANDS = 8
BLK_DEV = 128
BLOCKS = 1024
MOST = 32
KX = 17
KZ = 17


def draw_raw_views(key, part):
    key = jax.random.fold_in(key, 7)
    first = jax.random.fold_in(key, 0)
    shape = (VIEWS, BLOCKS, BAND, WY)
    values = jnp.exp(jax.random.uniform(first, shape, jnp.float32, jnp.log(0.3), jnp.log(3.0)))
    return values.astype(jnp.bfloat16)


def draw_block_dest(key, part):
    key = jax.random.fold_in(key, 11)
    slab_num = BLOCKS // BLK_DEV
    group = MOST // 2
    keys = jax.random.split(key, 3)
    offsets = jax.vmap(lambda inner: jax.random.permutation(inner, slab_num))(jax.random.split(keys[0], VIEWS))
    placing = jax.vmap(lambda inner: jax.random.permutation(inner, BLK_DEV))(jax.random.split(keys[1], VIEWS))
    ordering = jax.vmap(lambda inner: jax.random.permutation(inner, BLK_DEV))(jax.random.split(keys[2], VIEWS * slab_num))
    ordering = ordering.reshape(VIEWS, slab_num, BLK_DEV)
    groups = ordering // group
    groups = jnp.where(groups == 1, 0, groups)
    view_ids = jnp.arange(VIEWS)[:, None, None]
    shifted = offsets[view_ids, groups]
    sources = jnp.arange(slab_num)[None, :, None]
    target = (sources + shifted) % slab_num
    placed = placing[view_ids, ordering]
    return (target * BLK_DEV + placed).reshape(VIEWS, BLOCKS).astype(jnp.int32)


def shard_levels(stream_key, shape, shards, low, top_value):
    level, own = 1.0, jax.random.fold_in(stream_key, 6)
    for position, shards_of in shards:
        heights = jnp.exp(jax.random.uniform(jax.random.fold_in(own, position), (shards_of,), jnp.float32, low / len(shards), top_value / len(shards)))
        level = level * jnp.repeat(heights, shape[position] // shards_of).reshape([-1 if axis == position else 1 for axis in range(len(shape))])
    return level


def setup_inputs(seed: int = 0) -> dict:
    seeds = jax.random.split(jax.random.key(seed), 6)
    return {
        "estimate": jnp.clip(jnp.exp(math.log(2.0) - 1.3862944 * jax.random.uniform(seeds[0], (NZ, WX, WY), jnp.float32) ** shard_levels(seeds[0], (NZ, WX, WY), ((0, 8),), -0.2, 0.2)), 0.5, 2.0),
        "raw_views": draw_raw_views(jax.random.fold_in(seeds[5], 71), 0),
        "block_dest": draw_block_dest(jax.random.fold_in(seeds[5], 71), 0),
        "lateral_psf": jnp.clip(jnp.exp(math.log(1.0) - 2.9957323 * jax.random.uniform(seeds[3], (VIEWS, 2, KX), jnp.float32) ** shard_levels(seeds[3], (VIEWS, 2, KX), ((0, 4),), -0.2, 0.2)), 0.05, 1.0),
        "axial_psf": jnp.clip(jnp.exp(math.log(1.0) - 2.9957323 * jax.random.uniform(seeds[4], (VIEWS, KZ), jnp.float32) ** shard_levels(seeds[4], (VIEWS, KZ), ((0, 4),), -0.2, 0.2)), 0.05, 1.0),
    }


def normalize(kernel):
    return (kernel / jnp.sum(kernel, axis=-1, keepdims=True)).astype(jnp.bfloat16)


def band_matrix(kernel, extent):
    radius = (kernel.shape[-1] - 1) // 2
    places = jnp.arange(extent)
    offset = places[None, :] - places[:, None] + radius
    chosen = (offset[:, :, None] == jnp.arange(kernel.shape[-1])[None, None, :]).astype(jnp.float32)
    return jnp.einsum('ikw,w->ik', chosen, kernel.astype(jnp.float32))


def axial(volume, kernel, mirror):
    tap_num = kernel.shape[-1]
    radius = (tap_num - 1) // 2
    planes = volume.shape[0]
    padded = jnp.pad(volume, ((radius, radius), (0, 0), (0, 0)))
    summed = jnp.zeros(volume.shape, jnp.float32)
    for shift_idx in range(tap_num):
        weight_tap = kernel[tap_num - 1 - shift_idx] if mirror else kernel[shift_idx]
        summed = summed + weight_tap * padded[shift_idx:shift_idx + planes]
    return summed


def reference(estimate, raw_views, block_dest, lateral_psf, axial_psf):
    current = estimate
    for iteration in range(ITERS):
        lowered = current.astype(jnp.bfloat16)

        def one_view(summed, items):
            blocks, places, lateral, depth_taps = items
            observed = jnp.zeros((NZ * BANDS, BAND, WY), jnp.bfloat16).at[places].set(blocks).reshape(NZ, WX, WY)
            along_x = normalize(lateral[0])
            along_y = normalize(lateral[1])
            depth = normalize(depth_taps).astype(jnp.float32)
            mat_x = band_matrix(along_x, WX)
            mat_y = band_matrix(along_y, WY)
            first = axial(lowered.astype(jnp.float32), depth, False).astype(jnp.bfloat16)
            second = jnp.einsum('ik,zky->ziy', mat_x, first.astype(jnp.float32)).astype(jnp.bfloat16)
            blurred = jnp.einsum('zxl,jl->zxj', second.astype(jnp.float32), mat_y)
            ratio = (observed.astype(jnp.float32) / blurred).astype(jnp.bfloat16)
            third = jnp.einsum('zxj,jl->zxl', ratio.astype(jnp.float32), mat_y).astype(jnp.bfloat16)
            fourth = jnp.einsum('ik,ziy->zky', mat_x, third.astype(jnp.float32)).astype(jnp.bfloat16)
            return summed + axial(fourth.astype(jnp.float32), depth, True), None

        correction, unused = lax.scan(one_view, jnp.zeros((NZ, WX, WY), jnp.float32), (raw_views, block_dest, lateral_psf, axial_psf))
        current = current * correction / VIEWS
    return current
```

```python
import jax
import jax.numpy as jnp
from jax import lax
from jax.experimental import pallas as pl
from jax.experimental.pallas import tpu as pltpu
from jax.sharding import PartitionSpec as P

VIEWS = 12
ITERS = 2
VMEM_LIMIT = 48 * 1024 * 1024


def shift(array, axis, step):
    count = lax.axis_size(axis)
    if step > 0:
        pairs = [(i, i + 1) for i in range(count - 1)]
    else:
        pairs = [(i + 1, i) for i in range(count - 1)]
    return lax.ppermute(array, axis, pairs)


def normalize(kernel):
    return (kernel / jnp.sum(kernel, axis=-1, keepdims=True)).astype(jnp.bfloat16)


def band_matrix(kernel, extent):
    radius = (kernel.shape[-1] - 1) // 2
    places = jnp.arange(extent)
    offset = places[None, :] - places[:, None] + radius
    chosen = (offset[:, :, None] == jnp.arange(kernel.shape[-1])[None, None, :]).astype(jnp.float32)
    return jnp.einsum("ikw,vw->vik", chosen, kernel.astype(jnp.float32)).astype(jnp.bfloat16)


def axial_matrix(kernel, planes):
    tap_num = kernel.shape[-1]
    row_ids = jnp.arange(planes)[:, None]
    col_ids = jnp.arange(planes + tap_num - 1)[None, :]
    offset = col_ids - row_ids
    chosen = (offset[:, :, None] == jnp.arange(tap_num)[None, None, :]).astype(jnp.float32)
    return jnp.einsum("zpw,vw->vzp", chosen, kernel.astype(jnp.float32)).astype(jnp.bfloat16)


def pack_kernel(source, raw, packed, extra):
    slabs, views, group = packed.shape[:3]

    for v in range(views):

        @pl.loop(0, slabs)
        def _(s):
            for k in range(group):
                packed[s, v, k] = raw[v, source[v, s * group + k]]

        for k in range(group):
            extra[v, k] = raw[v, source[v, slabs * group + k]]


def pack(source, raw, slabs, group):
    views, _, band, rows_y = raw.shape
    vmem = pl.BlockSpec(memory_space=pltpu.VMEM)
    return pl.pallas_call(
        pack_kernel,
        out_shape=(
            jax.ShapeDtypeStruct((slabs, views, group, band, rows_y), raw.dtype),
            jax.ShapeDtypeStruct((views, group, band, rows_y), raw.dtype),
        ),
        in_specs=[pl.BlockSpec(memory_space=pltpu.SMEM), vmem],
        out_specs=(vmem, vmem),
        compiler_params=pltpu.CompilerParams(vmem_limit_bytes=VMEM_LIMIT),
        name="pack",
    )(source, raw)


def place_kernel(source, main, extra, blocks):
    views, num = blocks.shape[:2]
    unroll = 8

    for v in range(views):

        @pl.loop(0, num // unroll)
        def _(step):
            for k in range(unroll):
                q = step * unroll + k
                chosen = source[v, q]
                slab = chosen // 65536
                late = (chosen // 256) % 256
                slot = chosen % 256
                early_block = main[slab, v, slot]
                late_block = extra[slab, v, slot]
                blocks[v, q] = jnp.where(late == 1, late_block, early_block)


def place(source, main, extra):
    slabs, views, group, band, rows_y = main.shape
    vmem = pl.BlockSpec(memory_space=pltpu.VMEM)
    return pl.pallas_call(
        place_kernel,
        out_shape=jax.ShapeDtypeStruct((views, slabs * group, band, rows_y), main.dtype),
        in_specs=[pl.BlockSpec(memory_space=pltpu.SMEM), vmem, vmem],
        out_specs=vmem,
        compiler_params=pltpu.CompilerParams(vmem_limit_bytes=VMEM_LIMIT),
        name="place",
    )(source, main, extra)


def slots_of(dest, blk_num, slabs):
    target = dest // blk_num
    placed = dest % blk_num
    order = jnp.arange(blk_num)
    earlier = order[None, :] < order[:, None]
    same = (target[..., None, :] == target[..., :, None]) & earlier
    return target, placed, jnp.sum(same.astype(jnp.int32), axis=-1)


def route(raw_views, block_dest):
    view_num, blk_num = block_dest.shape
    slabs = lax.axis_size("gz")
    group = blk_num // slabs
    me = lax.axis_index("gz")
    target, placed, rank = slots_of(block_dest, blk_num, slabs)
    slot = jnp.where(rank < group, target * group + rank, slabs * group + rank - group)
    hit = slot[:, None, :] == jnp.arange((slabs + 1) * group)[None, :, None]
    source = jnp.sum(jnp.where(hit, jnp.arange(blk_num)[None, None, :], 0), axis=-1)
    packed, extra = pack(source, raw_views, slabs, group)
    main = lax.all_to_all(packed, "gz", split_axis=0, concat_axis=0, tiled=True)
    late = lax.all_gather(extra, "gz", axis=0)
    dests = lax.all_gather(block_dest, "gz", axis=0)
    target, placed, rank = slots_of(dests, blk_num, slabs)
    slab_ids = jnp.arange(slabs)[:, None, None]
    code = slab_ids * 65536 + jnp.where(rank < group, rank, 256 + rank - group)
    code = jnp.where(target == me, code, 0)
    code = jnp.swapaxes(code, 0, 1).reshape(view_num, slabs * blk_num)
    where = jnp.where(target == me, placed, blk_num)
    where = jnp.swapaxes(where, 0, 1).reshape(view_num, slabs * blk_num)
    hit = where[:, None, :] == jnp.arange(blk_num)[None, :, None]
    inverse = jnp.sum(jnp.where(hit, code[:, None, :], 0), axis=-1)
    return place(inverse, main, late)


def with_halo(quarter, radius):
    planes = quarter.shape[0]
    before = shift(quarter[planes - radius:], "gz", 1)
    after = shift(quarter[:radius], "gz", -1)
    return before, after


def body(estimate, raw_views, block_dest, lateral_psf, axial_psf):
    planes, rows_x, rows_y = estimate.shape
    along_x = normalize(lateral_psf[:, 0])
    along_y = normalize(lateral_psf[:, 1])
    depth = normalize(axial_psf)
    radius = (axial_psf.shape[1] - 1) // 2
    mat_x = band_matrix(along_x, rows_x)
    mat_y = band_matrix(along_y, rows_y)
    front_matrix = axial_matrix(depth, planes)
    parts = lax.axis_size("vert")
    rows_q = rows_x // parts
    mine = lax.axis_index("vert") * rows_q
    held = lax.dynamic_slice_in_dim(estimate, mine, rows_q, axis=1)
    before, after = with_halo(held.astype(jnp.bfloat16), radius)
    sides = lax.all_gather(jnp.concatenate([before, after], axis=0), "vert", axis=1, tiled=True)
    widened = jnp.concatenate(
        [sides[:radius], estimate.astype(jnp.bfloat16), sides[radius:]], axis=0
    )
    observed = route(raw_views, block_dest).reshape(-1, planes, rows_x, rows_y)
    for iteration in range(ITERS):
        first = jnp.einsum(
            "vzp,pxy->vzxy", front_matrix, widened, preferred_element_type=jnp.float32
        ).astype(jnp.bfloat16)
        second = jnp.einsum(
            "vik,vzky->vziy", mat_x, first, preferred_element_type=jnp.float32
        ).astype(jnp.bfloat16)
        blurred = jnp.einsum("vzxl,vjl->vzxj", second, mat_y, preferred_element_type=jnp.float32)
        ratio = (observed.astype(jnp.float32) / blurred).astype(jnp.bfloat16)
        third = jnp.einsum(
            "vzxj,vjl->vzxl", ratio, mat_y, preferred_element_type=jnp.float32
        ).astype(jnp.bfloat16)
        fourth = jnp.einsum(
            "vik,vziy->vzky", mat_x, third, preferred_element_type=jnp.float32
        ).astype(jnp.bfloat16)
        partial_back = jnp.einsum(
            "vzp,vzxy->pxy", front_matrix, fourth, preferred_element_type=jnp.float32
        )
        summed = lax.psum_scatter(partial_back, "vert", scatter_dimension=1, tiled=True)
        below = shift(summed[planes + radius:], "gz", 1)
        above = shift(summed[:radius], "gz", -1)
        correction = summed[radius:planes + radius] + jnp.concatenate([below, above], axis=0)
        held = held * correction / VIEWS
        if iteration < ITERS - 1:
            lowered = held.astype(jnp.bfloat16)
            before, after = with_halo(lowered, radius)
            widened = lax.all_gather(
                jnp.concatenate([before, lowered, after], axis=0), "vert", axis=1, tiled=True
            )
    return lax.all_gather(held, "vert", axis=1, tiled=True)


def solution(mesh):
    return jax.shard_map(
        body,
        mesh=mesh,
        in_specs=(
            P("gz", None, None),
            P("vert", "gz", None, None),
            P("vert", "gz"),
            P("vert", None, None),
            P("vert", None),
        ),
        out_specs=P("gz", None, None),
        check_vma=False,
    )
```

```python
import functools

import jax
import jax.numpy as jnp
from jax import lax
from jax.experimental import pallas as pl
from jax.experimental.pallas import tpu as pltpu
from jax.sharding import PartitionSpec as P

VIEWS = 12
ITERS = 2
VMEM_LIMIT = 48 * 1024 * 1024


def shift(array, axis, step):
    count = lax.axis_size(axis)
    if step > 0:
        pairs = [(i, i + 1) for i in range(count - 1)]
    else:
        pairs = [(i + 1, i) for i in range(count - 1)]
    return lax.ppermute(array, axis, pairs)


def normalize(kernel):
    return (kernel / jnp.sum(kernel, axis=-1, keepdims=True)).astype(jnp.bfloat16)


def band_matrix(kernel, extent):
    radius = (kernel.shape[-1] - 1) // 2
    places = jnp.arange(extent)
    offset = places[None, :] - places[:, None] + radius
    chosen = (offset[:, :, None] == jnp.arange(kernel.shape[-1])[None, None, :]).astype(jnp.float32)
    return jnp.einsum("ikw,vw->vik", chosen, kernel.astype(jnp.float32)).astype(jnp.bfloat16)


def axial_matrix(kernel, planes):
    tap_num = kernel.shape[-1]
    row_ids = jnp.arange(planes)[:, None]
    col_ids = jnp.arange(planes + tap_num - 1)[None, :]
    offset = col_ids - row_ids
    chosen = (offset[:, :, None] == jnp.arange(tap_num)[None, None, :]).astype(jnp.float32)
    return jnp.einsum("zpw,vw->vzp", chosen, kernel.astype(jnp.float32)).astype(jnp.bfloat16)


def pack_kernel(source, raw, packed, extra):
    slabs, views, group = packed.shape[:3]

    for v in range(views):

        @pl.loop(0, slabs)
        def _(s):
            for k in range(group):
                packed[s, v, k] = raw[v, source[v, s * group + k]]

        for k in range(group):
            extra[v, k] = raw[v, source[v, slabs * group + k]]


def pack(source, raw, slabs, group):
    views, _, band, rows_y = raw.shape
    vmem = pl.BlockSpec(memory_space=pltpu.VMEM)
    return pl.pallas_call(
        pack_kernel,
        out_shape=(
            jax.ShapeDtypeStruct((slabs, views, group, band, rows_y), raw.dtype),
            jax.ShapeDtypeStruct((views, group, band, rows_y), raw.dtype),
        ),
        in_specs=[pl.BlockSpec(memory_space=pltpu.SMEM), vmem],
        out_specs=(vmem, vmem),
        compiler_params=pltpu.CompilerParams(vmem_limit_bytes=VMEM_LIMIT),
        name="pack",
    )(source, raw)


def place_kernel(source, main, extra, blocks):
    views, num = blocks.shape[:2]
    unroll = 8

    for v in range(views):

        @pl.loop(0, num // unroll)
        def _(step):
            for k in range(unroll):
                q = step * unroll + k
                chosen = source[v, q]
                slab = chosen // 65536
                late = (chosen // 256) % 256
                slot = chosen % 256
                early_block = main[slab, v, slot]
                late_block = extra[slab, v, slot]
                blocks[v, q] = jnp.where(late == 1, late_block, early_block)


def place(source, main, extra):
    slabs, views, group, band, rows_y = main.shape
    vmem = pl.BlockSpec(memory_space=pltpu.VMEM)
    return pl.pallas_call(
        place_kernel,
        out_shape=jax.ShapeDtypeStruct((views, slabs * group, band, rows_y), main.dtype),
        in_specs=[pl.BlockSpec(memory_space=pltpu.SMEM), vmem, vmem],
        out_specs=vmem,
        compiler_params=pltpu.CompilerParams(vmem_limit_bytes=VMEM_LIMIT),
        name="place",
    )(source, main, extra)


def slots_of(dest, blk_num, slabs):
    target = dest // blk_num
    placed = dest % blk_num
    order = jnp.arange(blk_num)
    earlier = order[None, :] < order[:, None]
    same = (target[..., None, :] == target[..., :, None]) & earlier
    return target, placed, jnp.sum(same.astype(jnp.int32), axis=-1)


def route(raw_views, block_dest):
    view_num, blk_num = block_dest.shape
    slabs = lax.axis_size("gz")
    group = blk_num // slabs
    me = lax.axis_index("gz")
    dests = lax.all_gather(block_dest, "gz", axis=0)
    dests, block_dest = lax.optimization_barrier((dests, block_dest))
    target, placed, rank = slots_of(block_dest, blk_num, slabs)
    slot = jnp.where(rank < group, target * group + rank, slabs * group + rank - group)
    hit = slot[:, None, :] == jnp.arange((slabs + 1) * group)[None, :, None]
    source = jnp.sum(jnp.where(hit, jnp.arange(blk_num)[None, None, :], 0), axis=-1)
    packed, extra = pack(source, raw_views, slabs, group)
    main = lax.all_to_all(packed, "gz", split_axis=0, concat_axis=0, tiled=True)
    late = lax.all_gather(extra, "gz", axis=0)
    target, placed, rank = slots_of(dests, blk_num, slabs)
    slab_ids = jnp.arange(slabs)[:, None, None]
    code = slab_ids * 65536 + jnp.where(rank < group, rank, 256 + rank - group)
    code = jnp.where(target == me, code, 0)
    code = jnp.swapaxes(code, 0, 1).reshape(view_num, slabs * blk_num)
    where = jnp.where(target == me, placed, blk_num)
    where = jnp.swapaxes(where, 0, 1).reshape(view_num, slabs * blk_num)
    hit = where[:, None, :] == jnp.arange(blk_num)[None, :, None]
    inverse = jnp.sum(jnp.where(hit, code[:, None, :], 0), axis=-1)
    return place(inverse, main, late)


def exchange_kernel(last, partial, held, *refs):
    if last:
        (result, got_a, forward, got_b, edge, got_halo, send_sem, recv_sem) = refs
    else:
        (renewed, result, got_a, forward, got_b, edge, got_halo, send_sem, recv_sem) = refs
    planes, rows_q, _ = held.shape
    radius = edge.shape[1]
    half = planes // 2
    slab, slabs = lax.axis_index("gz"), lax.axis_size("gz")
    part, parts = lax.axis_index("vert"), lax.axis_size("vert")
    near = part + 1 - 2 * (part % 2)
    far = (part + 2) % parts
    near_far = (near + 2) % parts
    has_below, has_above = slab > 0, slab < slabs - 1
    taken = [0]

    def rows(quarter):
        return pl.ds(pl.multiple_of(quarter * rows_q, rows_q), rows_q)

    def remote(source, target, device):
        place = taken[0]
        taken[0] += 1
        return pltpu.make_async_remote_copy(
            src_ref=source,
            dst_ref=target,
            send_sem=send_sem.at[place],
            recv_sem=recv_sem.at[place],
            device_id=device,
            device_id_type=pl.DeviceIdType.MESH,
        )

    barrier = pltpu.get_barrier_semaphore()

    def greet(device):
        pl.semaphore_signal(barrier, inc=1, device_id=device, device_id_type=pl.DeviceIdType.MESH)

    greet({"vert": near})
    greet({"vert": far})
    pl.when(has_below)(lambda: greet({"gz": slab - 1}))
    pl.when(has_above)(lambda: greet({"gz": slab + 1}))
    pl.semaphore_wait(barrier, 2 + jnp.minimum(slab, 1) + jnp.minimum(slabs - 1 - slab, 1))

    chunks = [
        pl.ds(0, radius),
        pl.ds(planes + radius, radius),
        pl.ds(radius, half),
        pl.ds(radius + half, half),
    ]
    waits = []
    stage_a = []
    for chunk in chunks:
        passing = remote(partial.at[chunk, rows(near_far)], got_a.at[1, chunk], {"vert": near})
        passing.start()
        staying = remote(partial.at[chunk, rows(near)], got_a.at[0, chunk], {"vert": near})
        staying.start()
        stage_a.append((passing, staying))
        waits += [passing, staying]

    @pl.when(jnp.logical_not(has_below))
    def _():
        got_halo[0] = jnp.zeros(got_halo.shape[1:], got_halo.dtype)

    @pl.when(jnp.logical_not(has_above))
    def _():
        got_halo[1] = jnp.zeros(got_halo.shape[1:], got_halo.dtype)

    if not last:

        @pl.when(jnp.logical_not(has_below))
        def _():
            result[pl.ds(0, radius), rows(part)] = jnp.zeros(
                (radius, rows_q, result.shape[2]), result.dtype
            )

        @pl.when(jnp.logical_not(has_above))
        def _():
            result[pl.ds(planes + radius, radius), rows(part)] = jnp.zeros(
                (radius, rows_q, result.shape[2]), result.dtype
            )

    stage_b = []
    for chunk, (passing, _) in zip(chunks, stage_a):
        passing.wait_recv()
        forward[chunk] = partial[chunk, rows(far)] + got_a[1, chunk]
        copy = remote(forward.at[chunk], got_b.at[chunk], {"vert": far})
        copy.start()
        stage_b.append(copy)
        waits.append(copy)

    def total(place):
        chunk = chunks[place]
        stage_a[place][1].wait_recv()
        stage_b[place].wait_recv()
        return (partial[chunk, rows(part)] + got_a[0, chunk]) + got_b[chunk]

    edge[0] = total(0)
    down = remote(edge.at[0], got_halo.at[1], {"gz": slab - 1})
    pl.when(has_below)(lambda: down.start())
    edge[1] = total(1)
    up = remote(edge.at[1], got_halo.at[0], {"gz": slab + 1})
    pl.when(has_above)(lambda: up.start())

    inner = 0 if last else radius
    shared = []
    besides = []
    moved = []
    for place in range(2):
        summed = total(2 + place)
        if place == 0:
            pl.when(has_below)(lambda: up.wait_recv())
        else:
            pl.when(has_above)(lambda: down.wait_recv())
        own = pl.ds(place * half, half)
        value = held[own] * (summed + got_halo[place]) / VIEWS
        if not last:
            renewed[own] = value
        target = result.at[pl.ds(inner + place * half, half), rows(part)]
        target[...] = value.astype(result.dtype)
        if not last:
            if place == 0:
                copy = remote(
                    target, result.at[pl.ds(planes + radius, radius), rows(part)], {"gz": slab - 1}
                )
                pl.when(has_below)(functools.partial(copy.start))
            else:
                copy = remote(target, result.at[pl.ds(0, radius), rows(part)], {"gz": slab + 1})
                pl.when(has_above)(functools.partial(copy.start))
            moved.append(copy)
        across = remote(target, target, {"vert": far})
        across.start()
        beside = remote(target, target, {"vert": near})
        beside.start()
        shared.append((inner + place * half, half, across))
        waits += [across, beside]
        besides.append(beside)
    late = []

    def relay(start, length, across):
        across.wait_recv()
        target = result.at[pl.ds(start, length), rows(far)]
        copy = remote(target, target, {"vert": near})
        copy.start()
        late.append(copy)

    if last:
        for item in shared:
            relay(*item)
    else:
        relay(*shared[0])
        relay(*shared[1])
        outer = []
        for place in range(2):
            start = planes + radius if place == 0 else 0
            pl.when(has_above if place == 0 else has_below)(
                functools.partial(moved[place].wait_recv)
            )
            target = result.at[pl.ds(start, radius), rows(part)]
            across = remote(target, target, {"vert": far})
            across.start()
            beside = remote(target, target, {"vert": near})
            beside.start()
            outer.append((start, radius, across))
            late.append(beside)
        for item in outer:
            relay(*item)
            waits.append(item[2])
        pl.when(has_below)(lambda: moved[0].wait_send())
        pl.when(has_above)(lambda: moved[1].wait_send())
    pl.when(has_below)(lambda: down.wait_send())
    pl.when(has_above)(lambda: up.wait_send())
    for copy in waits:
        copy.wait_send()
    for copy in late:
        copy.wait_send()
        copy.wait_recv()
    for copy in besides:
        copy.wait_recv()


def exchange(partial, held, last):
    whole, rows_x, rows_y = partial.shape
    planes, rows_q, _ = held.shape
    radius = (whole - planes) // 2
    assert planes == 2 * radius and rows_x == 4 * rows_q
    vmem = pl.BlockSpec(memory_space=pltpu.VMEM)
    f32 = jnp.float32
    if last:
        out_shape = jax.ShapeDtypeStruct((planes, rows_x, rows_y), f32)
        out_specs = vmem
    else:
        out_shape = (
            jax.ShapeDtypeStruct(held.shape, f32),
            jax.ShapeDtypeStruct((whole, rows_x, rows_y), jnp.bfloat16),
        )
        out_specs = (vmem, vmem)
    copies = 20 if last else 28
    return pl.pallas_call(
        functools.partial(exchange_kernel, last),
        out_shape=out_shape,
        in_specs=[vmem, vmem],
        out_specs=out_specs,
        scratch_shapes=[
            pltpu.VMEM((2, whole, rows_q, rows_y), f32),
            pltpu.VMEM((whole, rows_q, rows_y), f32),
            pltpu.VMEM((whole, rows_q, rows_y), f32),
            pltpu.VMEM((2, radius, rows_q, rows_y), f32),
            pltpu.VMEM((2, radius, rows_q, rows_y), f32),
            pltpu.SemaphoreType.DMA((copies,)),
            pltpu.SemaphoreType.DMA((copies,)),
        ],
        compiler_params=pltpu.CompilerParams(
            collective_id=1 if last else 0, has_side_effects=True, vmem_limit_bytes=VMEM_LIMIT
        ),
        name="finish" if last else "renew",
    )(partial, held)


def halo_of(quarter, radius):
    planes = quarter.shape[0]
    return shift(quarter[planes - radius:], "gz", 1), shift(quarter[:radius], "gz", -1)


def body(estimate, raw_views, block_dest, lateral_psf, axial_psf):
    planes, rows_x, rows_y = estimate.shape
    along_x = normalize(lateral_psf[:, 0])
    along_y = normalize(lateral_psf[:, 1])
    depth = normalize(axial_psf)
    radius = (axial_psf.shape[1] - 1) // 2
    mat_x = band_matrix(along_x, rows_x)
    mat_y = band_matrix(along_y, rows_y)
    front_matrix = axial_matrix(depth, planes)
    parts = lax.axis_size("vert")
    rows_q = rows_x // parts
    mine = lax.axis_index("vert") * rows_q
    held = lax.dynamic_slice_in_dim(estimate, mine, rows_q, axis=1)
    before, after = halo_of(held.astype(jnp.bfloat16), radius)
    sides = lax.all_gather(jnp.concatenate([before, after], axis=0), "vert", axis=1, tiled=True)
    widened = jnp.concatenate(
        [sides[:radius], estimate.astype(jnp.bfloat16), sides[radius:]], axis=0
    )
    observed = route(raw_views, block_dest).reshape(-1, planes, rows_x, rows_y)
    for iteration in range(ITERS):
        first = jnp.einsum(
            "vzp,pxy->vzxy", front_matrix, widened, preferred_element_type=jnp.float32
        ).astype(jnp.bfloat16)
        second = jnp.einsum(
            "vik,vzky->vziy", mat_x, first, preferred_element_type=jnp.float32
        ).astype(jnp.bfloat16)
        blurred = jnp.einsum("vzxl,vjl->vzxj", second, mat_y, preferred_element_type=jnp.float32)
        ratio = (observed.astype(jnp.float32) / blurred).astype(jnp.bfloat16)
        third = jnp.einsum(
            "vzxj,vjl->vzxl", ratio, mat_y, preferred_element_type=jnp.float32
        ).astype(jnp.bfloat16)
        fourth = jnp.einsum(
            "vik,vziy->vzky", mat_x, third, preferred_element_type=jnp.float32
        ).astype(jnp.bfloat16)
        partial_back = jnp.einsum(
            "vzp,vzxy->pxy", front_matrix, fourth, preferred_element_type=jnp.float32
        )
        if iteration < ITERS - 1:
            held, widened = exchange(partial_back, held, False)
        else:
            held = exchange(partial_back, held, True)
    return held


def solution(mesh):
    return jax.shard_map(
        body,
        mesh=mesh,
        in_specs=(
            P("gz", None, None),
            P("vert", "gz", None, None),
            P("vert", "gz"),
            P("vert", None, None),
            P("vert", None),
        ),
        out_specs=P("gz", None, None),
        check_vma=False,
    )
```

```python
import functools

import jax
import jax.numpy as jnp
from jax import lax
from jax.experimental import pallas as pl
from jax.experimental.pallas import tpu as pltpu
from jax.sharding import PartitionSpec as P

VIEWS = 12
ITERS = 2
VMEM_LIMIT = 48 * 1024 * 1024


def normalize(kernel):
    return (kernel / jnp.sum(kernel, axis=-1, keepdims=True)).astype(jnp.bfloat16)


def band_matrix(kernel, extent):
    radius = (kernel.shape[-1] - 1) // 2
    places = jnp.arange(extent)
    offset = places[None, :] - places[:, None] + radius
    chosen = (offset[:, :, None] == jnp.arange(kernel.shape[-1])[None, None, :]).astype(jnp.float32)
    return jnp.einsum("ikw,vw->vik", chosen, kernel.astype(jnp.float32)).astype(jnp.bfloat16)


def axial_matrix(kernel, planes):
    tap_num = kernel.shape[-1]
    row_ids = jnp.arange(planes)[:, None]
    col_ids = jnp.arange(planes + tap_num - 1)[None, :]
    offset = col_ids - row_ids
    chosen = (offset[:, :, None] == jnp.arange(tap_num)[None, None, :]).astype(jnp.float32)
    return jnp.einsum("zpw,vw->vzp", chosen, kernel.astype(jnp.float32)).astype(jnp.bfloat16)


def pack_kernel(source, raw, packed, extra):
    slabs, views, group = packed.shape[:3]

    for v in range(views):

        @pl.loop(0, slabs)
        def _(s):
            for k in range(group):
                packed[s, v, k] = raw[v, source[v, s * group + k]]

        for k in range(group):
            extra[v, k] = raw[v, source[v, slabs * group + k]]


def pack(source, raw, slabs, group):
    views, _, band, rows_y = raw.shape
    vmem = pl.BlockSpec(memory_space=pltpu.VMEM)
    return pl.pallas_call(
        pack_kernel,
        out_shape=(
            jax.ShapeDtypeStruct((slabs, views, group, band, rows_y), raw.dtype),
            jax.ShapeDtypeStruct((views, group, band, rows_y), raw.dtype),
        ),
        in_specs=[pl.BlockSpec(memory_space=pltpu.SMEM), vmem],
        out_specs=(vmem, vmem),
        compiler_params=pltpu.CompilerParams(vmem_limit_bytes=VMEM_LIMIT),
        name="pack",
    )(source, raw)


def spread_kernel(estimate, extra, dest, widened, late, dests, send_sem, recv_sem):
    planes, rows_x, rows_y = estimate.shape
    radius = (widened.shape[0] - planes) // 2
    slab, slabs = lax.axis_index("gz"), lax.axis_size("gz")
    part, parts = lax.axis_index("vert"), lax.axis_size("vert")
    rows_q = rows_x // parts
    near = part + 1 - 2 * (part % 2)
    far = (part + 2) % parts
    lines = slabs // 2
    line, side = slab // 2, slab % 2
    other = slab + 1 - 2 * side
    has_below, has_above = slab > 0, slab < slabs - 1
    line_below, line_above = line > 0, line < lines - 1
    taken = [0]

    def rows(quarter):
        return pl.ds(pl.multiple_of(quarter * rows_q, rows_q), rows_q)

    def remote(source, target, device):
        place = taken[0]
        taken[0] += 1
        return pltpu.make_async_remote_copy(
            src_ref=source,
            dst_ref=target,
            send_sem=send_sem.at[place],
            recv_sem=recv_sem.at[place],
            device_id=device,
            device_id_type=pl.DeviceIdType.MESH,
        )

    def groups(index, device):
        return (
            remote(late.at[index], late.at[index], device),
            remote(dests.at[index], dests.at[index], device),
        )

    def start(copies):
        for copy in copies:
            copy.start()

    def wait_recv(copies):
        for copy in copies:
            copy.wait_recv()

    def wait_send(copies):
        for copy in copies:
            copy.wait_send()

    barrier = pltpu.get_barrier_semaphore()

    def greet(device):
        pl.semaphore_signal(barrier, inc=1, device_id=device, device_id_type=pl.DeviceIdType.MESH)

    greet({"vert": near})
    greet({"vert": far})
    pl.when(has_below)(lambda: greet({"gz": slab - 1}))
    pl.when(has_above)(lambda: greet({"gz": slab + 1}))
    pl.when(line_below)(lambda: greet({"gz": slab - 2}))
    pl.when(line_above)(lambda: greet({"gz": slab + 2}))
    pl.semaphore_wait(
        barrier,
        2
        + jnp.minimum(slab, 1)
        + jnp.minimum(slabs - 1 - slab, 1)
        + jnp.minimum(line, 1)
        + jnp.minimum(lines - 1 - line, 1),
    )

    for edge in (0, planes - radius):
        widened[pl.ds(radius + edge, radius), rows(part)] = estimate[
            pl.ds(edge, radius), rows(part)
        ].astype(widened.dtype)
    lowest = widened.at[pl.ds(radius, radius), rows(part)]
    highest = widened.at[pl.ds(planes, radius), rows(part)]
    before = widened.at[pl.ds(0, radius), rows(part)]
    after = widened.at[pl.ds(planes + radius, radius), rows(part)]
    down = remote(lowest, after, {"gz": slab - 1})
    up = remote(highest, before, {"gz": slab + 1})
    pl.when(has_below)(down.start)
    pl.when(has_above)(up.start)

    late[slab] = extra[...]
    dests[slab] = dest[...]
    swaps = [(None, groups(slab, {"gz": other}))]
    rising, falling = [], []
    for step in range(lines - 1):
        index = jnp.maximum(line - step, 0) * 2 + side
        rising.append((line_above & (line >= step), groups(index, {"gz": slab + 2})))
        index = jnp.minimum(line + step, lines - 1) * 2 + side
        falling.append((line_below & (line + step < lines), groups(index, {"gz": slab - 2})))
    pl.when(rising[0][0])(lambda: start(rising[0][1]))
    pl.when(falling[0][0])(lambda: start(falling[0][1]))
    start(swaps[0][1])

    @pl.when(jnp.logical_not(has_below))
    def _():
        before[...] = jnp.zeros(before.shape, before.dtype)

    @pl.when(jnp.logical_not(has_above))
    def _():
        after[...] = jnp.zeros(after.shape, after.dtype)

    half = rows_x // parts
    for quarter in range(parts):
        own = pl.ds(quarter * half, half)

        @pl.when(part != quarter)
        def _():
            widened[pl.ds(radius, planes), own] = estimate[:, own].astype(widened.dtype)

    middle = planes - 2 * radius
    if middle:
        widened[pl.ds(2 * radius, middle), rows(part)] = estimate[
            pl.ds(radius, middle), rows(part)
        ].astype(widened.dtype)

    sides = []
    for start_plane, landed, copy, exists in (
        (0, before, up, has_below),
        (planes + radius, after, down, has_above),
    ):
        pl.when(exists)(copy.wait_recv)
        across = remote(landed, landed, {"vert": far})
        across.start()
        beside = remote(landed, landed, {"vert": near})
        beside.start()
        sides.append((start_plane, across, beside))
    relays = []
    for start_plane, across, beside in sides:
        across.wait_recv()
        landed = widened.at[pl.ds(start_plane, radius), rows(far)]
        copy = remote(landed, landed, {"vert": near})
        copy.start()
        relays.append(copy)

    for step in range(lines - 1):
        came = line >= step + 1
        index = jnp.maximum(line - 1 - step, 0) * 2 + side
        swap = groups(index, {"gz": other})
        pl.when(came)(lambda: wait_recv(rising[step][1]))
        if step + 1 < lines - 1:
            pl.when(rising[step + 1][0])(lambda: start(rising[step + 1][1]))
        pl.when(came)(lambda: start(swap))
        swaps.append((came, swap))
        came = line + 1 + step < lines
        index = jnp.minimum(line + 1 + step, lines - 1) * 2 + side
        swap = groups(index, {"gz": other})
        pl.when(came)(lambda: wait_recv(falling[step][1]))
        if step + 1 < lines - 1:
            pl.when(falling[step + 1][0])(lambda: start(falling[step + 1][1]))
        pl.when(came)(lambda: start(swap))
        swaps.append((came, swap))

    pl.when(has_below)(down.wait_send)
    pl.when(has_above)(up.wait_send)
    for _, across, beside in sides:
        across.wait_send()
        beside.wait()
    for copy in relays:
        copy.wait()
    for sent, copies in rising + falling:
        pl.when(sent)(lambda: wait_send(copies))
    for came, copies in swaps:
        if came is None:
            wait_send(copies)
            wait_recv(copies)
        else:
            pl.when(came)(lambda: wait_send(copies))
            pl.when(came)(lambda: wait_recv(copies))


def spread(estimate, extra, dest, radius):
    planes, rows_x, rows_y = estimate.shape
    slabs = lax.axis_size("gz")
    copies = 8 + 2 * (1 + 4 * (slabs // 2 - 1))
    vmem = pl.BlockSpec(memory_space=pltpu.VMEM)
    return pl.pallas_call(
        spread_kernel,
        out_shape=(
            jax.ShapeDtypeStruct((planes + 2 * radius, rows_x, rows_y), jnp.bfloat16),
            jax.ShapeDtypeStruct((slabs,) + extra.shape, extra.dtype),
            jax.ShapeDtypeStruct((slabs,) + dest.shape, dest.dtype),
        ),
        in_specs=[vmem] * 3,
        out_specs=(vmem,) * 3,
        scratch_shapes=[
            pltpu.SemaphoreType.DMA((copies,)),
            pltpu.SemaphoreType.DMA((copies,)),
        ],
        compiler_params=pltpu.CompilerParams(
            collective_id=2, has_side_effects=True, vmem_limit_bytes=VMEM_LIMIT
        ),
        cost_estimate=pl.CostEstimate(flops=0, bytes_accessed=120000000, transcendentals=0),
        name="spread",
    )(estimate, extra, dest)


def place_kernel(source, main, extra, blocks):
    views, num = blocks.shape[:2]
    unroll = 8

    for v in range(views):

        @pl.loop(0, num // unroll)
        def _(step):
            for k in range(unroll):
                q = step * unroll + k
                chosen = source[v, q]
                slab = chosen // 65536
                late = (chosen // 256) % 256
                slot = chosen % 256
                early_block = main[slab, v, slot]
                late_block = extra[slab, v, slot]
                blocks[v, q] = jnp.where(late == 1, late_block, early_block)


def place(source, main, extra):
    slabs, views, group, band, rows_y = main.shape
    vmem = pl.BlockSpec(memory_space=pltpu.VMEM)
    return pl.pallas_call(
        place_kernel,
        out_shape=jax.ShapeDtypeStruct((views, slabs * group, band, rows_y), main.dtype),
        in_specs=[pl.BlockSpec(memory_space=pltpu.SMEM), vmem, vmem],
        out_specs=vmem,
        compiler_params=pltpu.CompilerParams(vmem_limit_bytes=VMEM_LIMIT),
        name="place",
    )(source, main, extra)


def slots_of(dest, blk_num, slabs):
    target = dest // blk_num
    placed = dest % blk_num
    order = jnp.arange(blk_num)
    earlier = order[None, :] < order[:, None]
    same = (target[..., None, :] == target[..., :, None]) & earlier
    return target, placed, jnp.sum(same.astype(jnp.int32), axis=-1)


def source_of(block_dest):
    blk_num = block_dest.shape[1]
    slabs = lax.axis_size("gz")
    group = blk_num // slabs
    target, _, rank = slots_of(block_dest, blk_num, slabs)
    slot = jnp.where(rank < group, target * group + rank, slabs * group + rank - group)
    hit = slot[:, None, :] == jnp.arange((slabs + 1) * group)[None, :, None]
    return jnp.sum(jnp.where(hit, jnp.arange(blk_num)[None, None, :], 0), axis=-1)


def origin_of(dests):
    slabs, view_num, blk_num = dests.shape
    group = blk_num // slabs
    me = lax.axis_index("gz")
    target, placed, rank = slots_of(dests, blk_num, slabs)
    slab_ids = jnp.arange(slabs)[:, None, None]
    code = slab_ids * 65536 + jnp.where(rank < group, rank, 256 + rank - group)
    code = jnp.where(target == me, code, 0)
    code = jnp.swapaxes(code, 0, 1).reshape(view_num, slabs * blk_num)
    where = jnp.where(target == me, placed, blk_num)
    where = jnp.swapaxes(where, 0, 1).reshape(view_num, slabs * blk_num)
    hit = where[:, None, :] == jnp.arange(blk_num)[None, :, None]
    return jnp.sum(jnp.where(hit, code[:, None, :], 0), axis=-1)


def exchange_kernel(last, partial, held, *refs):
    if last:
        (result, got_a, forward, got_b, edge, got_halo, send_sem, recv_sem) = refs
    else:
        (renewed, result, got_a, forward, got_b, edge, got_halo, send_sem, recv_sem) = refs
    planes, rows_q, _ = held.shape
    radius = edge.shape[1]
    half = planes // 2
    slab, slabs = lax.axis_index("gz"), lax.axis_size("gz")
    part, parts = lax.axis_index("vert"), lax.axis_size("vert")
    near = part + 1 - 2 * (part % 2)
    far = (part + 2) % parts
    near_far = (near + 2) % parts
    has_below, has_above = slab > 0, slab < slabs - 1
    taken = [0]

    def rows(quarter):
        return pl.ds(pl.multiple_of(quarter * rows_q, rows_q), rows_q)

    def remote(source, target, device):
        place = taken[0]
        taken[0] += 1
        return pltpu.make_async_remote_copy(
            src_ref=source,
            dst_ref=target,
            send_sem=send_sem.at[place],
            recv_sem=recv_sem.at[place],
            device_id=device,
            device_id_type=pl.DeviceIdType.MESH,
        )

    barrier = pltpu.get_barrier_semaphore()

    def greet(device):
        pl.semaphore_signal(barrier, inc=1, device_id=device, device_id_type=pl.DeviceIdType.MESH)

    greet({"vert": near})
    greet({"vert": far})
    pl.when(has_below)(lambda: greet({"gz": slab - 1}))
    pl.when(has_above)(lambda: greet({"gz": slab + 1}))
    pl.semaphore_wait(barrier, 2 + jnp.minimum(slab, 1) + jnp.minimum(slabs - 1 - slab, 1))

    chunks = [
        pl.ds(0, radius),
        pl.ds(planes + radius, radius),
        pl.ds(radius, half),
        pl.ds(radius + half, half),
    ]
    waits = []
    stage_a = []
    for chunk in chunks:
        passing = remote(partial.at[chunk, rows(near_far)], got_a.at[1, chunk], {"vert": near})
        passing.start()
        staying = remote(partial.at[chunk, rows(near)], got_a.at[0, chunk], {"vert": near})
        staying.start()
        stage_a.append((passing, staying))
        waits += [passing, staying]

    @pl.when(jnp.logical_not(has_below))
    def _():
        got_halo[0] = jnp.zeros(got_halo.shape[1:], got_halo.dtype)

    @pl.when(jnp.logical_not(has_above))
    def _():
        got_halo[1] = jnp.zeros(got_halo.shape[1:], got_halo.dtype)

    if not last:

        @pl.when(jnp.logical_not(has_below))
        def _():
            result[pl.ds(0, radius), rows(part)] = jnp.zeros(
                (radius, rows_q, result.shape[2]), result.dtype
            )

        @pl.when(jnp.logical_not(has_above))
        def _():
            result[pl.ds(planes + radius, radius), rows(part)] = jnp.zeros(
                (radius, rows_q, result.shape[2]), result.dtype
            )

    stage_b = []
    for chunk, (passing, _) in zip(chunks, stage_a):
        passing.wait_recv()
        forward[chunk] = partial[chunk, rows(far)] + got_a[1, chunk]
        copy = remote(forward.at[chunk], got_b.at[chunk], {"vert": far})
        copy.start()
        stage_b.append(copy)
        waits.append(copy)

    def total(place):
        chunk = chunks[place]
        stage_a[place][1].wait_recv()
        stage_b[place].wait_recv()
        return (partial[chunk, rows(part)] + got_a[0, chunk]) + got_b[chunk]

    edge[0] = total(0)
    down = remote(edge.at[0], got_halo.at[1], {"gz": slab - 1})
    pl.when(has_below)(lambda: down.start())
    edge[1] = total(1)
    up = remote(edge.at[1], got_halo.at[0], {"gz": slab + 1})
    pl.when(has_above)(lambda: up.start())

    inner = 0 if last else radius
    shared = []
    besides = []
    moved = []
    for place in range(2):
        summed = total(2 + place)
        if place == 0:
            pl.when(has_below)(lambda: up.wait_recv())
        else:
            pl.when(has_above)(lambda: down.wait_recv())
        own = pl.ds(place * half, half)
        value = held[own] * (summed + got_halo[place]) / VIEWS
        if not last:
            renewed[own] = value
        target = result.at[pl.ds(inner + place * half, half), rows(part)]
        target[...] = value.astype(result.dtype)
        if not last:
            if place == 0:
                copy = remote(
                    target, result.at[pl.ds(planes + radius, radius), rows(part)], {"gz": slab - 1}
                )
                pl.when(has_below)(functools.partial(copy.start))
            else:
                copy = remote(target, result.at[pl.ds(0, radius), rows(part)], {"gz": slab + 1})
                pl.when(has_above)(functools.partial(copy.start))
            moved.append(copy)
        across = remote(target, target, {"vert": far})
        across.start()
        beside = remote(target, target, {"vert": near})
        beside.start()
        shared.append((inner + place * half, half, across))
        waits += [across, beside]
        besides.append(beside)
    late = []

    def relay(start, length, across):
        across.wait_recv()
        target = result.at[pl.ds(start, length), rows(far)]
        copy = remote(target, target, {"vert": near})
        copy.start()
        late.append(copy)

    if last:
        for item in shared:
            relay(*item)
    else:
        relay(*shared[0])
        relay(*shared[1])
        outer = []
        for place in range(2):
            start = planes + radius if place == 0 else 0
            pl.when(has_above if place == 0 else has_below)(
                functools.partial(moved[place].wait_recv)
            )
            target = result.at[pl.ds(start, radius), rows(part)]
            across = remote(target, target, {"vert": far})
            across.start()
            beside = remote(target, target, {"vert": near})
            beside.start()
            outer.append((start, radius, across))
            late.append(beside)
        for item in outer:
            relay(*item)
            waits.append(item[2])
        pl.when(has_below)(lambda: moved[0].wait_send())
        pl.when(has_above)(lambda: moved[1].wait_send())
    pl.when(has_below)(lambda: down.wait_send())
    pl.when(has_above)(lambda: up.wait_send())
    for copy in waits:
        copy.wait_send()
    for copy in late:
        copy.wait_send()
        copy.wait_recv()
    for copy in besides:
        copy.wait_recv()


def exchange(partial, held, last):
    whole, rows_x, rows_y = partial.shape
    planes, rows_q, _ = held.shape
    radius = (whole - planes) // 2
    assert planes == 2 * radius and rows_x == 4 * rows_q
    vmem = pl.BlockSpec(memory_space=pltpu.VMEM)
    f32 = jnp.float32
    if last:
        out_shape = jax.ShapeDtypeStruct((planes, rows_x, rows_y), f32)
        out_specs = vmem
    else:
        out_shape = (
            jax.ShapeDtypeStruct(held.shape, f32),
            jax.ShapeDtypeStruct((whole, rows_x, rows_y), jnp.bfloat16),
        )
        out_specs = (vmem, vmem)
    copies = 20 if last else 28
    return pl.pallas_call(
        functools.partial(exchange_kernel, last),
        out_shape=out_shape,
        in_specs=[vmem, vmem],
        out_specs=out_specs,
        scratch_shapes=[
            pltpu.VMEM((2, whole, rows_q, rows_y), f32),
            pltpu.VMEM((whole, rows_q, rows_y), f32),
            pltpu.VMEM((whole, rows_q, rows_y), f32),
            pltpu.VMEM((2, radius, rows_q, rows_y), f32),
            pltpu.VMEM((2, radius, rows_q, rows_y), f32),
            pltpu.SemaphoreType.DMA((copies,)),
            pltpu.SemaphoreType.DMA((copies,)),
        ],
        compiler_params=pltpu.CompilerParams(
            collective_id=1 if last else 0, has_side_effects=True, vmem_limit_bytes=VMEM_LIMIT
        ),
        name="finish" if last else "renew",
    )(partial, held)


def body(estimate, raw_views, block_dest, lateral_psf, axial_psf):
    planes, rows_x, rows_y = estimate.shape
    along_x = normalize(lateral_psf[:, 0])
    along_y = normalize(lateral_psf[:, 1])
    depth = normalize(axial_psf)
    radius = (axial_psf.shape[1] - 1) // 2
    mat_x = band_matrix(along_x, rows_x)
    mat_y = band_matrix(along_y, rows_y)
    front_matrix = axial_matrix(depth, planes)
    parts = lax.axis_size("vert")
    rows_q = rows_x // parts
    mine = lax.axis_index("vert") * rows_q
    held = lax.dynamic_slice_in_dim(estimate, mine, rows_q, axis=1)
    slabs = lax.axis_size("gz")
    packed, extra = pack(source_of(block_dest), raw_views, slabs, block_dest.shape[1] // slabs)
    main = lax.all_to_all(packed, "gz", split_axis=0, concat_axis=0, tiled=True)
    widened, late, dests = spread(estimate, extra, block_dest, radius)
    observed = place(origin_of(dests), main, late).reshape(-1, planes, rows_x, rows_y)
    for iteration in range(ITERS):
        first = jnp.einsum(
            "vzp,pxy->vzxy", front_matrix, widened, preferred_element_type=jnp.float32
        ).astype(jnp.bfloat16)
        second = jnp.einsum(
            "vik,vzky->vziy", mat_x, first, preferred_element_type=jnp.float32
        ).astype(jnp.bfloat16)
        blurred = jnp.einsum("vzxl,vjl->vzxj", second, mat_y, preferred_element_type=jnp.float32)
        ratio = (observed.astype(jnp.float32) / blurred).astype(jnp.bfloat16)
        third = jnp.einsum(
            "vzxj,vjl->vzxl", ratio, mat_y, preferred_element_type=jnp.float32
        ).astype(jnp.bfloat16)
        fourth = jnp.einsum(
            "vik,vziy->vzky", mat_x, third, preferred_element_type=jnp.float32
        ).astype(jnp.bfloat16)
        partial_back = jnp.einsum(
            "vzp,vzxy->pxy", front_matrix, fourth, preferred_element_type=jnp.float32
        )
        if iteration < ITERS - 1:
            held, widened = exchange(partial_back, held, False)
        else:
            held = exchange(partial_back, held, True)
    return held


def solution(mesh):
    return jax.shard_map(
        body,
        mesh=mesh,
        in_specs=(
            P("gz", None, None),
            P("vert", "gz", None, None),
            P("vert", "gz"),
            P("vert", None, None),
            P("vert", None),
        ),
        out_specs=P("gz", None, None),
        check_vma=False,
    )
```

```python
import functools

import jax
import jax.numpy as jnp
from jax import lax
from jax.experimental import pallas as pl
from jax.experimental.pallas import tpu as pltpu
from jax.sharding import PartitionSpec as P

VIEWS = 12
ITERS = 2
VMEM_LIMIT = 48 * 1024 * 1024


def normalize(kernel):
    return (kernel / jnp.sum(kernel, axis=-1, keepdims=True)).astype(jnp.bfloat16)


def band_matrix(kernel, extent):
    radius = (kernel.shape[-1] - 1) // 2
    places = jnp.arange(extent)
    offset = places[None, :] - places[:, None] + radius
    chosen = (offset[:, :, None] == jnp.arange(kernel.shape[-1])[None, None, :]).astype(jnp.float32)
    return jnp.einsum("ikw,vw->vik", chosen, kernel.astype(jnp.float32)).astype(jnp.bfloat16)


def axial_matrix(kernel, planes):
    tap_num = kernel.shape[-1]
    row_ids = jnp.arange(planes)[:, None]
    col_ids = jnp.arange(planes + tap_num - 1)[None, :]
    offset = col_ids - row_ids
    chosen = (offset[:, :, None] == jnp.arange(tap_num)[None, None, :]).astype(jnp.float32)
    return jnp.einsum("zpw,vw->vzp", chosen, kernel.astype(jnp.float32)).astype(jnp.bfloat16)


def pack_kernel(source, raw, packed, extra):
    slabs, views, group = packed.shape[:3]

    for v in range(views):

        @pl.loop(0, slabs)
        def _(s):
            for k in range(group):
                packed[s, v, k] = raw[v, source[v, s * group + k]]

        for k in range(group):
            extra[v, k] = raw[v, source[v, slabs * group + k]]


def pack(source, raw, slabs, group):
    views, _, band, rows_y = raw.shape
    vmem = pl.BlockSpec(memory_space=pltpu.VMEM)
    return pl.pallas_call(
        pack_kernel,
        out_shape=(
            jax.ShapeDtypeStruct((slabs, views, group, band, rows_y), raw.dtype),
            jax.ShapeDtypeStruct((views, group, band, rows_y), raw.dtype),
        ),
        in_specs=[pl.BlockSpec(memory_space=pltpu.SMEM), vmem],
        out_specs=(vmem, vmem),
        compiler_params=pltpu.CompilerParams(vmem_limit_bytes=VMEM_LIMIT),
        name="pack",
    )(source, raw)


def spread_kernel(
    estimate, packed, extra, dest, widened, main, late, dests, send_sem, recv_sem
):
    planes, rows_x, rows_y = estimate.shape
    radius = (widened.shape[0] - planes) // 2
    slab, slabs = lax.axis_index("gz"), lax.axis_size("gz")
    part, parts = lax.axis_index("vert"), lax.axis_size("vert")
    rows_q = rows_x // parts
    near = part + 1 - 2 * (part % 2)
    far = (part + 2) % parts
    lines = slabs // 2
    line, side = slab // 2, slab % 2
    other = slab + 1 - 2 * side
    has_below, has_above = slab > 0, slab < slabs - 1
    line_below, line_above = line > 0, line < lines - 1
    taken = [0]

    def rows(quarter):
        return pl.ds(pl.multiple_of(quarter * rows_q, rows_q), rows_q)

    def remote(source, target, device):
        place = taken[0]
        taken[0] += 1
        return pltpu.make_async_remote_copy(
            src_ref=source,
            dst_ref=target,
            send_sem=send_sem.at[place],
            recv_sem=recv_sem.at[place],
            device_id=device,
            device_id_type=pl.DeviceIdType.MESH,
        )

    def groups(index, device):
        return (
            remote(late.at[index], late.at[index], device),
            remote(dests.at[index], dests.at[index], device),
        )

    def start(copies):
        for copy in copies:
            copy.start()

    def wait_recv(copies):
        for copy in copies:
            copy.wait_recv()

    def wait_send(copies):
        for copy in copies:
            copy.wait_send()

    barrier = pltpu.get_barrier_semaphore()

    def greet(device):
        pl.semaphore_signal(barrier, inc=1, device_id=device, device_id_type=pl.DeviceIdType.MESH)

    greet({"vert": near})
    greet({"vert": far})

    def peer(distance):
        found, bit = slab, 1
        while bit < slabs:
            if distance & bit:
                found = found + bit - 2 * bit * ((slab // bit) % 2)
            bit *= 2
        return found

    for distance in range(1, slabs):
        greet({"gz": peer(distance)})
    pl.semaphore_wait(barrier, slabs + 1)

    for edge in (0, planes - radius):
        widened[pl.ds(radius + edge, radius), rows(part)] = estimate[
            pl.ds(edge, radius), rows(part)
        ].astype(widened.dtype)
    lowest = widened.at[pl.ds(radius, radius), rows(part)]
    highest = widened.at[pl.ds(planes, radius), rows(part)]
    before = widened.at[pl.ds(0, radius), rows(part)]
    after = widened.at[pl.ds(planes + radius, radius), rows(part)]
    down = remote(lowest, after, {"gz": slab - 1})
    up = remote(highest, before, {"gz": slab + 1})
    pl.when(has_below)(down.start)
    pl.when(has_above)(up.start)

    late[slab] = extra[...]
    dests[slab] = dest[...]
    swaps = [(None, groups(slab, {"gz": other}))]
    rising, falling = [], []
    for step in range(lines - 1):
        index = jnp.maximum(line - step, 0) * 2 + side
        rising.append((line_above & (line >= step), groups(index, {"gz": slab + 2})))
        index = jnp.minimum(line + step, lines - 1) * 2 + side
        falling.append((line_below & (line + step < lines), groups(index, {"gz": slab - 2})))
    pl.when(rising[0][0])(lambda: start(rising[0][1]))
    pl.when(falling[0][0])(lambda: start(falling[0][1]))
    start(swaps[0][1])

    groups_sent = []
    for distance in range(slabs - 1, 0, -1):
        copy = remote(packed.at[peer(distance)], main.at[slab], {"gz": peer(distance)})
        copy.start()
        groups_sent.append(copy)
    main[slab] = packed[slab]

    @pl.when(jnp.logical_not(has_below))
    def _():
        before[...] = jnp.zeros(before.shape, before.dtype)

    @pl.when(jnp.logical_not(has_above))
    def _():
        after[...] = jnp.zeros(after.shape, after.dtype)

    half = rows_x // parts
    for quarter in range(parts):
        own = pl.ds(quarter * half, half)

        @pl.when(part != quarter)
        def _():
            widened[pl.ds(radius, planes), own] = estimate[:, own].astype(widened.dtype)

    middle = planes - 2 * radius
    if middle:
        widened[pl.ds(2 * radius, middle), rows(part)] = estimate[
            pl.ds(radius, middle), rows(part)
        ].astype(widened.dtype)

    sides = []
    for start_plane, landed, copy, exists in (
        (0, before, up, has_below),
        (planes + radius, after, down, has_above),
    ):
        pl.when(exists)(copy.wait_recv)
        across = remote(landed, landed, {"vert": far})
        across.start()
        beside = remote(landed, landed, {"vert": near})
        beside.start()
        sides.append((start_plane, across, beside))
    relays = []
    for start_plane, across, beside in sides:
        across.wait_recv()
        landed = widened.at[pl.ds(start_plane, radius), rows(far)]
        copy = remote(landed, landed, {"vert": near})
        copy.start()
        relays.append(copy)

    for step in range(lines - 1):
        came = line >= step + 1
        index = jnp.maximum(line - 1 - step, 0) * 2 + side
        swap = groups(index, {"gz": other})
        pl.when(came)(lambda: wait_recv(rising[step][1]))
        if step + 1 < lines - 1:
            pl.when(rising[step + 1][0])(lambda: start(rising[step + 1][1]))
        pl.when(came)(lambda: start(swap))
        swaps.append((came, swap))
        came = line + 1 + step < lines
        index = jnp.minimum(line + 1 + step, lines - 1) * 2 + side
        swap = groups(index, {"gz": other})
        pl.when(came)(lambda: wait_recv(falling[step][1]))
        if step + 1 < lines - 1:
            pl.when(falling[step + 1][0])(lambda: start(falling[step + 1][1]))
        pl.when(came)(lambda: start(swap))
        swaps.append((came, swap))

    pl.when(has_below)(down.wait_send)
    pl.when(has_above)(up.wait_send)
    for _, across, beside in sides:
        across.wait_send()
        beside.wait()
    for copy in relays:
        copy.wait()
    for sent, copies in rising + falling:
        pl.when(sent)(lambda: wait_send(copies))
    for came, copies in swaps:
        if came is None:
            wait_send(copies)
            wait_recv(copies)
        else:
            pl.when(came)(lambda: wait_send(copies))
            pl.when(came)(lambda: wait_recv(copies))
    for copy in groups_sent:
        copy.wait_send()
        copy.wait_recv()


def spread(estimate, packed, extra, dest, radius):
    planes, rows_x, rows_y = estimate.shape
    slabs = lax.axis_size("gz")
    copies = 8 + 2 * (1 + 4 * (slabs // 2 - 1)) + slabs - 1
    vmem = pl.BlockSpec(memory_space=pltpu.VMEM)
    return pl.pallas_call(
        spread_kernel,
        out_shape=(
            jax.ShapeDtypeStruct((planes + 2 * radius, rows_x, rows_y), jnp.bfloat16),
            jax.ShapeDtypeStruct(packed.shape, packed.dtype),
            jax.ShapeDtypeStruct((slabs,) + extra.shape, extra.dtype),
            jax.ShapeDtypeStruct((slabs,) + dest.shape, dest.dtype),
        ),
        in_specs=[vmem] * 4,
        out_specs=(vmem,) * 4,
        scratch_shapes=[
            pltpu.SemaphoreType.DMA((copies,)),
            pltpu.SemaphoreType.DMA((copies,)),
        ],
        compiler_params=pltpu.CompilerParams(
            collective_id=2, has_side_effects=True, vmem_limit_bytes=VMEM_LIMIT
        ),
        name="spread",
    )(estimate, packed, extra, dest)


def place_kernel(source, main, extra, blocks):
    views, num = blocks.shape[:2]
    unroll = 8

    for v in range(views):

        @pl.loop(0, num // unroll)
        def _(step):
            for k in range(unroll):
                q = step * unroll + k
                chosen = source[v, q]
                slab = chosen // 65536
                late = (chosen // 256) % 256
                slot = chosen % 256
                early_block = main[slab, v, slot]
                late_block = extra[slab, v, slot]
                blocks[v, q] = jnp.where(late == 1, late_block, early_block)


def place(source, main, extra):
    slabs, views, group, band, rows_y = main.shape
    vmem = pl.BlockSpec(memory_space=pltpu.VMEM)
    return pl.pallas_call(
        place_kernel,
        out_shape=jax.ShapeDtypeStruct((views, slabs * group, band, rows_y), main.dtype),
        in_specs=[pl.BlockSpec(memory_space=pltpu.SMEM), vmem, vmem],
        out_specs=vmem,
        compiler_params=pltpu.CompilerParams(vmem_limit_bytes=VMEM_LIMIT),
        name="place",
    )(source, main, extra)


def slots_of(dest, blk_num, slabs):
    target = dest // blk_num
    placed = dest % blk_num
    order = jnp.arange(blk_num)
    earlier = order[None, :] < order[:, None]
    same = (target[..., None, :] == target[..., :, None]) & earlier
    return target, placed, jnp.sum(same.astype(jnp.int32), axis=-1)


def source_of(block_dest):
    blk_num = block_dest.shape[1]
    slabs = lax.axis_size("gz")
    group = blk_num // slabs
    target, _, rank = slots_of(block_dest, blk_num, slabs)
    slot = jnp.where(rank < group, target * group + rank, slabs * group + rank - group)
    hit = slot[:, None, :] == jnp.arange((slabs + 1) * group)[None, :, None]
    return jnp.sum(jnp.where(hit, jnp.arange(blk_num)[None, None, :], 0), axis=-1)


def origin_of(dests):
    slabs, view_num, blk_num = dests.shape
    group = blk_num // slabs
    me = lax.axis_index("gz")
    target, placed, rank = slots_of(dests, blk_num, slabs)
    slab_ids = jnp.arange(slabs)[:, None, None]
    code = slab_ids * 65536 + jnp.where(rank < group, rank, 256 + rank - group)
    code = jnp.where(target == me, code, 0)
    code = jnp.swapaxes(code, 0, 1).reshape(view_num, slabs * blk_num)
    where = jnp.where(target == me, placed, blk_num)
    where = jnp.swapaxes(where, 0, 1).reshape(view_num, slabs * blk_num)
    hit = where[:, None, :] == jnp.arange(blk_num)[None, :, None]
    return jnp.sum(jnp.where(hit, code[:, None, :], 0), axis=-1)


def exchange_kernel(last, partial, held, *refs):
    if last:
        (result, got_a, forward, got_b, edge, got_halo, send_sem, recv_sem) = refs
    else:
        (renewed, result, got_a, forward, got_b, edge, got_halo, send_sem, recv_sem) = refs
    planes, rows_q, _ = held.shape
    radius = edge.shape[2]
    half = planes // 2
    slab, slabs = lax.axis_index("gz"), lax.axis_size("gz")
    part, parts = lax.axis_index("vert"), lax.axis_size("vert")
    near = part + 1 - 2 * (part % 2)
    far = (part + 2) % parts
    near_far = (near + 2) % parts
    has_below, has_above = slab > 0, slab < slabs - 1
    taken = [0]

    def rows(quarter):
        return pl.ds(pl.multiple_of(quarter * rows_q, rows_q), rows_q)

    def remote(source, target, device):
        place = taken[0]
        taken[0] += 1
        return pltpu.make_async_remote_copy(
            src_ref=source,
            dst_ref=target,
            send_sem=send_sem.at[place],
            recv_sem=recv_sem.at[place],
            device_id=device,
            device_id_type=pl.DeviceIdType.MESH,
        )

    barrier = pltpu.get_barrier_semaphore()

    def greet(device):
        pl.semaphore_signal(barrier, inc=1, device_id=device, device_id_type=pl.DeviceIdType.MESH)

    greet({"vert": near})
    greet({"vert": far})
    pl.when(has_below)(lambda: greet({"gz": slab - 1}))
    pl.when(has_above)(lambda: greet({"gz": slab + 1}))
    pl.semaphore_wait(barrier, 2 + jnp.minimum(slab, 1) + jnp.minimum(slabs - 1 - slab, 1))

    chunks = [
        pl.ds(0, radius),
        pl.ds(planes + radius, radius),
        pl.ds(radius, half),
        pl.ds(radius + half, half),
    ]
    waits = []
    stage_a = []
    for chunk in chunks:
        passing = remote(partial.at[rows(near_far), chunk], got_a.at[1, :, chunk], {"vert": near})
        passing.start()
        staying = remote(partial.at[rows(near), chunk], got_a.at[0, :, chunk], {"vert": near})
        staying.start()
        stage_a.append((passing, staying))
        waits += [passing, staying]

    @pl.when(jnp.logical_not(has_below))
    def _():
        got_halo[0] = jnp.zeros(got_halo.shape[1:], got_halo.dtype)

    @pl.when(jnp.logical_not(has_above))
    def _():
        got_halo[1] = jnp.zeros(got_halo.shape[1:], got_halo.dtype)

    if not last:

        @pl.when(jnp.logical_not(has_below))
        def _():
            result[pl.ds(0, radius), rows(part)] = jnp.zeros(
                (radius, rows_q, result.shape[2]), result.dtype
            )

        @pl.when(jnp.logical_not(has_above))
        def _():
            result[pl.ds(planes + radius, radius), rows(part)] = jnp.zeros(
                (radius, rows_q, result.shape[2]), result.dtype
            )

    stage_b = []
    for chunk, (passing, _) in zip(chunks, stage_a):
        passing.wait_recv()
        forward[:, chunk] = partial[rows(far), chunk] + got_a[1, :, chunk]
        copy = remote(forward.at[:, chunk], got_b.at[:, chunk], {"vert": far})
        copy.start()
        stage_b.append(copy)
        waits.append(copy)

    def total(place):
        chunk = chunks[place]
        stage_a[place][1].wait_recv()
        stage_b[place].wait_recv()
        return (partial[rows(part), chunk] + got_a[0, :, chunk]) + got_b[:, chunk]

    edge[0] = total(0)
    down = remote(edge.at[0], got_halo.at[1], {"gz": slab - 1})
    pl.when(has_below)(lambda: down.start())
    edge[1] = total(1)
    up = remote(edge.at[1], got_halo.at[0], {"gz": slab + 1})
    pl.when(has_above)(lambda: up.start())

    inner = 0 if last else radius
    shared = []
    besides = []
    moved = []
    for place in range(2):
        summed = total(2 + place)
        if place == 0:
            pl.when(has_below)(lambda: up.wait_recv())
        else:
            pl.when(has_above)(lambda: down.wait_recv())
        own = pl.ds(place * half, half)
        value = held[own] * jnp.swapaxes(summed + got_halo[place], 0, 1) / VIEWS
        if not last:
            renewed[own] = value
        target = result.at[pl.ds(inner + place * half, half), rows(part)]
        target[...] = value.astype(result.dtype)
        if not last:
            if place == 0:
                copy = remote(
                    target, result.at[pl.ds(planes + radius, radius), rows(part)], {"gz": slab - 1}
                )
                pl.when(has_below)(functools.partial(copy.start))
            else:
                copy = remote(target, result.at[pl.ds(0, radius), rows(part)], {"gz": slab + 1})
                pl.when(has_above)(functools.partial(copy.start))
            moved.append(copy)
        across = remote(target, target, {"vert": far})
        across.start()
        beside = remote(target, target, {"vert": near})
        beside.start()
        shared.append((inner + place * half, half, across))
        waits += [across, beside]
        besides.append(beside)
    late = []

    def relay(start, length, across):
        across.wait_recv()
        target = result.at[pl.ds(start, length), rows(far)]
        copy = remote(target, target, {"vert": near})
        copy.start()
        late.append(copy)

    if last:
        for item in shared:
            relay(*item)
    else:
        relay(*shared[0])
        relay(*shared[1])
        outer = []
        for place in range(2):
            start = planes + radius if place == 0 else 0
            pl.when(has_above if place == 0 else has_below)(
                functools.partial(moved[place].wait_recv)
            )
            target = result.at[pl.ds(start, radius), rows(part)]
            across = remote(target, target, {"vert": far})
            across.start()
            beside = remote(target, target, {"vert": near})
            beside.start()
            outer.append((start, radius, across))
            late.append(beside)
        for item in outer:
            relay(*item)
            waits.append(item[2])
        pl.when(has_below)(lambda: moved[0].wait_send())
        pl.when(has_above)(lambda: moved[1].wait_send())
    pl.when(has_below)(lambda: down.wait_send())
    pl.when(has_above)(lambda: up.wait_send())
    for copy in waits:
        copy.wait_send()
    for copy in late:
        copy.wait_send()
        copy.wait_recv()
    for copy in besides:
        copy.wait_recv()


def exchange(partial, held, last):
    rows_x, whole, rows_y = partial.shape
    planes, rows_q, _ = held.shape
    radius = (whole - planes) // 2
    assert planes == 2 * radius and rows_x == 4 * rows_q
    vmem = pl.BlockSpec(memory_space=pltpu.VMEM)
    f32 = jnp.float32
    if last:
        out_shape = jax.ShapeDtypeStruct((planes, rows_x, rows_y), f32)
        out_specs = vmem
    else:
        out_shape = (
            jax.ShapeDtypeStruct(held.shape, f32),
            jax.ShapeDtypeStruct((whole, rows_x, rows_y), jnp.bfloat16),
        )
        out_specs = (vmem, vmem)
    copies = 20 if last else 28
    return pl.pallas_call(
        functools.partial(exchange_kernel, last),
        out_shape=out_shape,
        in_specs=[vmem, vmem],
        out_specs=out_specs,
        scratch_shapes=[
            pltpu.VMEM((2, rows_q, whole, rows_y), f32),
            pltpu.VMEM((rows_q, whole, rows_y), f32),
            pltpu.VMEM((rows_q, whole, rows_y), f32),
            pltpu.VMEM((2, rows_q, radius, rows_y), f32),
            pltpu.VMEM((2, rows_q, radius, rows_y), f32),
            pltpu.SemaphoreType.DMA((copies,)),
            pltpu.SemaphoreType.DMA((copies,)),
        ],
        compiler_params=pltpu.CompilerParams(
            collective_id=1 if last else 0, has_side_effects=True, vmem_limit_bytes=VMEM_LIMIT
        ),
        name="finish" if last else "renew",
    )(partial, held)


def body(estimate, raw_views, block_dest, lateral_psf, axial_psf):
    planes, rows_x, rows_y = estimate.shape
    along_x = normalize(lateral_psf[:, 0])
    along_y = normalize(lateral_psf[:, 1])
    depth = normalize(axial_psf)
    radius = (axial_psf.shape[1] - 1) // 2
    mat_x = band_matrix(along_x, rows_x)
    mat_y = band_matrix(along_y, rows_y)
    front_matrix = axial_matrix(depth, planes)
    parts = lax.axis_size("vert")
    rows_q = rows_x // parts
    mine = lax.axis_index("vert") * rows_q
    held = lax.dynamic_slice_in_dim(estimate, mine, rows_q, axis=1)
    slabs = lax.axis_size("gz")
    packed, extra = pack(source_of(block_dest), raw_views, slabs, block_dest.shape[1] // slabs)
    widened, main, late, dests = spread(estimate, packed, extra, block_dest, radius)
    observed = place(origin_of(dests), main, late).reshape(-1, planes, rows_x, rows_y)
    for iteration in range(ITERS):
        first = jnp.einsum(
            "vzp,pxy->vzxy", front_matrix, widened, preferred_element_type=jnp.float32
        ).astype(jnp.bfloat16)
        second = jnp.einsum(
            "vik,vzky->vziy", mat_x, first, preferred_element_type=jnp.float32
        ).astype(jnp.bfloat16)
        blurred = jnp.einsum("vzxl,vjl->vzxj", second, mat_y, preferred_element_type=jnp.float32)
        ratio = (observed.astype(jnp.float32) / blurred).astype(jnp.bfloat16)
        third = jnp.einsum(
            "vzxj,vjl->vzxl", ratio, mat_y, preferred_element_type=jnp.float32
        ).astype(jnp.bfloat16)
        fourth = jnp.einsum(
            "vik,vziy->vzky", mat_x, third, preferred_element_type=jnp.float32
        ).astype(jnp.bfloat16)
        partial_back = jnp.einsum(
            "vzp,vzxy->xpy", front_matrix, fourth, preferred_element_type=jnp.float32
        )
        if iteration < ITERS - 1:
            held, widened = exchange(partial_back, held, False)
        else:
            held = exchange(partial_back, held, True)
    return held


def solution(mesh):
    return jax.shard_map(
        body,
        mesh=mesh,
        in_specs=(
            P("gz", None, None),
            P("vert", "gz", None, None),
            P("vert", "gz"),
            P("vert", None, None),
            P("vert", None),
        ),
        out_specs=P("gz", None, None),
        check_vma=False,
    )
```

```python
import functools

import jax
import jax.numpy as jnp
from jax import lax
from jax.experimental import pallas as pl
from jax.experimental.pallas import tpu as pltpu
from jax.sharding import PartitionSpec as P

VIEWS = 12
ITERS = 2
VMEM_LIMIT = 48 * 1024 * 1024


def normalize(kernel):
    return (kernel / jnp.sum(kernel, axis=-1, keepdims=True)).astype(jnp.bfloat16)


def band_matrix(kernel, extent):
    radius = (kernel.shape[-1] - 1) // 2
    places = jnp.arange(extent)
    offset = places[None, :] - places[:, None] + radius
    chosen = (offset[:, :, None] == jnp.arange(kernel.shape[-1])[None, None, :]).astype(jnp.float32)
    return jnp.einsum("ikw,vw->vik", chosen, kernel.astype(jnp.float32)).astype(jnp.bfloat16)


def axial_matrix(kernel, planes):
    tap_num = kernel.shape[-1]
    row_ids = jnp.arange(planes)[:, None]
    col_ids = jnp.arange(planes + tap_num - 1)[None, :]
    offset = col_ids - row_ids
    chosen = (offset[:, :, None] == jnp.arange(tap_num)[None, None, :]).astype(jnp.float32)
    return jnp.einsum("zpw,vw->vzp", chosen, kernel.astype(jnp.float32)).astype(jnp.bfloat16)


def pack_kernel(source, raw, packed, extra):
    slabs, views, group = packed.shape[:3]

    for v in range(views):

        @pl.loop(0, slabs)
        def _(s):
            for k in range(group):
                packed[s, v, k] = raw[v, source[v, s * group + k]]

        for k in range(group):
            extra[v, k] = raw[v, source[v, slabs * group + k]]


def pack(source, raw, slabs, group):
    views, _, band, rows_y = raw.shape
    vmem = pl.BlockSpec(memory_space=pltpu.VMEM)
    return pl.pallas_call(
        pack_kernel,
        out_shape=(
            jax.ShapeDtypeStruct((slabs, views, group, band, rows_y), raw.dtype),
            jax.ShapeDtypeStruct((views, group, band, rows_y), raw.dtype),
        ),
        in_specs=[pl.BlockSpec(memory_space=pltpu.SMEM), vmem],
        out_specs=(vmem, vmem),
        compiler_params=pltpu.CompilerParams(vmem_limit_bytes=VMEM_LIMIT),
        name="pack",
    )(source, raw)


def spread_kernel(
    estimate, packed, extra, dest, widened, main, late, dests, send_sem, recv_sem
):
    planes, rows_x, rows_y = estimate.shape
    radius = (widened.shape[0] - planes) // 2
    slab, slabs = lax.axis_index("gz"), lax.axis_size("gz")
    part, parts = lax.axis_index("vert"), lax.axis_size("vert")
    rows_q = rows_x // parts
    near = part + 1 - 2 * (part % 2)
    far = (part + 2) % parts
    lines = slabs // 2
    line, side = slab // 2, slab % 2
    other = slab + 1 - 2 * side
    has_below, has_above = slab > 0, slab < slabs - 1
    line_below, line_above = line > 0, line < lines - 1
    taken = [0]

    def rows(quarter):
        return pl.ds(pl.multiple_of(quarter * rows_q, rows_q), rows_q)

    def remote(source, target, device):
        place = taken[0]
        taken[0] += 1
        return pltpu.make_async_remote_copy(
            src_ref=source,
            dst_ref=target,
            send_sem=send_sem.at[place],
            recv_sem=recv_sem.at[place],
            device_id=device,
            device_id_type=pl.DeviceIdType.MESH,
        )

    def groups(index, device):
        return (
            remote(late.at[index], late.at[index], device),
            remote(dests.at[index], dests.at[index], device),
        )

    def start(copies):
        for copy in copies:
            copy.start()

    def wait_recv(copies):
        for copy in copies:
            copy.wait_recv()

    def wait_send(copies):
        for copy in copies:
            copy.wait_send()

    barrier = pltpu.get_barrier_semaphore()

    def greet(device):
        pl.semaphore_signal(barrier, inc=1, device_id=device, device_id_type=pl.DeviceIdType.MESH)

    greet({"vert": near})
    greet({"vert": far})

    def peer(distance):
        found, bit = slab, 1
        while bit < slabs:
            if distance & bit:
                found = found + bit - 2 * bit * ((slab // bit) % 2)
            bit *= 2
        return found

    for distance in range(1, slabs):
        greet({"gz": peer(distance)})
    pl.semaphore_wait(barrier, slabs + 1)

    for edge in (0, planes - radius):
        widened[pl.ds(radius + edge, radius), rows(part)] = estimate[
            pl.ds(edge, radius), rows(part)
        ].astype(widened.dtype)
    lowest = widened.at[pl.ds(radius, radius), rows(part)]
    highest = widened.at[pl.ds(planes, radius), rows(part)]
    before = widened.at[pl.ds(0, radius), rows(part)]
    after = widened.at[pl.ds(planes + radius, radius), rows(part)]
    down = remote(lowest, after, {"gz": slab - 1})
    up = remote(highest, before, {"gz": slab + 1})
    pl.when(has_below)(down.start)
    pl.when(has_above)(up.start)

    late[slab] = extra[...]
    dests[slab] = dest[...]
    swaps = [(None, groups(slab, {"gz": other}))]
    rising, falling = [], []
    for step in range(lines - 1):
        index = jnp.maximum(line - step, 0) * 2 + side
        rising.append((line_above & (line >= step), groups(index, {"gz": slab + 2})))
        index = jnp.minimum(line + step, lines - 1) * 2 + side
        falling.append((line_below & (line + step < lines), groups(index, {"gz": slab - 2})))
    pl.when(rising[0][0])(lambda: start(rising[0][1]))
    pl.when(falling[0][0])(lambda: start(falling[0][1]))
    start(swaps[0][1])

    groups_sent = []
    for distance in range(slabs - 1, 0, -1):
        groups_sent.append(
            remote(packed.at[peer(distance)], main.at[slab], {"gz": peer(distance)})
        )
    groups_sent[0].start()
    main[slab] = packed[slab]

    @pl.when(jnp.logical_not(has_below))
    def _():
        before[...] = jnp.zeros(before.shape, before.dtype)

    @pl.when(jnp.logical_not(has_above))
    def _():
        after[...] = jnp.zeros(after.shape, after.dtype)

    half = rows_x // parts
    for quarter in range(parts):
        own = pl.ds(quarter * half, half)

        @pl.when(part != quarter)
        def _():
            widened[pl.ds(radius, planes), own] = estimate[:, own].astype(widened.dtype)

    middle = planes - 2 * radius
    if middle:
        widened[pl.ds(2 * radius, middle), rows(part)] = estimate[
            pl.ds(radius, middle), rows(part)
        ].astype(widened.dtype)

    sides = []
    for start_plane, landed, copy, exists in (
        (0, before, up, has_below),
        (planes + radius, after, down, has_above),
    ):
        pl.when(exists)(copy.wait_recv)
        across = remote(landed, landed, {"vert": far})
        across.start()
        beside = remote(landed, landed, {"vert": near})
        beside.start()
        sides.append((start_plane, across, beside))
    relays = []
    for start_plane, across, beside in sides:
        across.wait_recv()
        landed = widened.at[pl.ds(start_plane, radius), rows(far)]
        copy = remote(landed, landed, {"vert": near})
        copy.start()
        relays.append(copy)

    for step in range(lines - 1):
        came = line >= step + 1
        index = jnp.maximum(line - 1 - step, 0) * 2 + side
        swap = groups(index, {"gz": other})
        pl.when(came)(lambda: wait_recv(rising[step][1]))
        if step + 1 < lines - 1:
            pl.when(rising[step + 1][0])(lambda: start(rising[step + 1][1]))
        pl.when(came)(lambda: start(swap))
        swaps.append((came, swap))
        came = line + 1 + step < lines
        index = jnp.minimum(line + 1 + step, lines - 1) * 2 + side
        swap = groups(index, {"gz": other})
        pl.when(came)(lambda: wait_recv(falling[step][1]))
        if step + 1 < lines - 1:
            pl.when(falling[step + 1][0])(lambda: start(falling[step + 1][1]))
        pl.when(came)(lambda: start(swap))
        swaps.append((came, swap))
        if step + 1 < lines - 1:
            groups_sent[step + 1].start()
        else:
            start(groups_sent[step + 1:])

    pl.when(has_below)(down.wait_send)
    pl.when(has_above)(up.wait_send)
    for _, across, beside in sides:
        across.wait_send()
        beside.wait()
    for copy in relays:
        copy.wait()
    for sent, copies in rising + falling:
        pl.when(sent)(lambda: wait_send(copies))
    for came, copies in swaps:
        if came is None:
            wait_send(copies)
            wait_recv(copies)
        else:
            pl.when(came)(lambda: wait_send(copies))
            pl.when(came)(lambda: wait_recv(copies))
    for copy in groups_sent:
        copy.wait_send()
        copy.wait_recv()


def spread(estimate, packed, extra, dest, radius):
    planes, rows_x, rows_y = estimate.shape
    slabs = lax.axis_size("gz")
    copies = 8 + 2 * (1 + 4 * (slabs // 2 - 1)) + slabs - 1
    vmem = pl.BlockSpec(memory_space=pltpu.VMEM)
    return pl.pallas_call(
        spread_kernel,
        out_shape=(
            jax.ShapeDtypeStruct((planes + 2 * radius, rows_x, rows_y), jnp.bfloat16),
            jax.ShapeDtypeStruct(packed.shape, packed.dtype),
            jax.ShapeDtypeStruct((slabs,) + extra.shape, extra.dtype),
            jax.ShapeDtypeStruct((slabs,) + dest.shape, dest.dtype),
        ),
        in_specs=[vmem] * 4,
        out_specs=(vmem,) * 4,
        scratch_shapes=[
            pltpu.SemaphoreType.DMA((copies,)),
            pltpu.SemaphoreType.DMA((copies,)),
        ],
        compiler_params=pltpu.CompilerParams(
            collective_id=2, has_side_effects=True, vmem_limit_bytes=VMEM_LIMIT
        ),
        name="spread",
    )(estimate, packed, extra, dest)


def place_kernel(source, main, extra, blocks):
    views, num = blocks.shape[:2]
    unroll = 8

    for v in range(views):

        @pl.loop(0, num // unroll)
        def _(step):
            for k in range(unroll):
                q = step * unroll + k
                chosen = source[v, q]
                slab = chosen // 65536
                late = (chosen // 256) % 256
                slot = chosen % 256
                early_block = main[slab, v, slot]
                late_block = extra[slab, v, slot]
                blocks[v, q] = jnp.where(late == 1, late_block, early_block)


def place(source, main, extra):
    slabs, views, group, band, rows_y = main.shape
    vmem = pl.BlockSpec(memory_space=pltpu.VMEM)
    return pl.pallas_call(
        place_kernel,
        out_shape=jax.ShapeDtypeStruct((views, slabs * group, band, rows_y), main.dtype),
        in_specs=[pl.BlockSpec(memory_space=pltpu.SMEM), vmem, vmem],
        out_specs=vmem,
        compiler_params=pltpu.CompilerParams(vmem_limit_bytes=VMEM_LIMIT),
        name="place",
    )(source, main, extra)


def slots_of(dest, blk_num, slabs):
    target = dest // blk_num
    placed = dest % blk_num
    order = jnp.arange(blk_num)
    earlier = order[None, :] < order[:, None]
    same = (target[..., None, :] == target[..., :, None]) & earlier
    return target, placed, jnp.sum(same.astype(jnp.int32), axis=-1)


def source_of(block_dest):
    blk_num = block_dest.shape[1]
    slabs = lax.axis_size("gz")
    group = blk_num // slabs
    target, _, rank = slots_of(block_dest, blk_num, slabs)
    slot = jnp.where(rank < group, target * group + rank, slabs * group + rank - group)
    hit = slot[:, None, :] == jnp.arange((slabs + 1) * group)[None, :, None]
    return jnp.sum(jnp.where(hit, jnp.arange(blk_num)[None, None, :], 0), axis=-1)


def origin_of(dests):
    slabs, view_num, blk_num = dests.shape
    group = blk_num // slabs
    me = lax.axis_index("gz")
    target, placed, rank = slots_of(dests, blk_num, slabs)
    slab_ids = jnp.arange(slabs)[:, None, None]
    code = slab_ids * 65536 + jnp.where(rank < group, rank, 256 + rank - group)
    code = jnp.where(target == me, code, 0)
    code = jnp.swapaxes(code, 0, 1).reshape(view_num, slabs * blk_num)
    where = jnp.where(target == me, placed, blk_num)
    where = jnp.swapaxes(where, 0, 1).reshape(view_num, slabs * blk_num)
    hit = where[:, None, :] == jnp.arange(blk_num)[None, :, None]
    return jnp.sum(jnp.where(hit, code[:, None, :], 0), axis=-1)


def exchange_kernel(last, partial, held, *refs):
    if last:
        (result, got_a, forward, got_b, edge, got_halo, send_sem, recv_sem) = refs
    else:
        (renewed, result, got_a, forward, got_b, edge, got_halo, send_sem, recv_sem) = refs
    planes, rows_q, _ = held.shape
    radius = edge.shape[2]
    half = planes // 2
    slab, slabs = lax.axis_index("gz"), lax.axis_size("gz")
    part, parts = lax.axis_index("vert"), lax.axis_size("vert")
    near = part + 1 - 2 * (part % 2)
    far = (part + 2) % parts
    near_far = (near + 2) % parts
    has_below, has_above = slab > 0, slab < slabs - 1
    taken = [0]

    def rows(quarter):
        return pl.ds(pl.multiple_of(quarter * rows_q, rows_q), rows_q)

    def remote(source, target, device):
        place = taken[0]
        taken[0] += 1
        return pltpu.make_async_remote_copy(
            src_ref=source,
            dst_ref=target,
            send_sem=send_sem.at[place],
            recv_sem=recv_sem.at[place],
            device_id=device,
            device_id_type=pl.DeviceIdType.MESH,
        )

    barrier = pltpu.get_barrier_semaphore()

    def greet(device):
        pl.semaphore_signal(barrier, inc=1, device_id=device, device_id_type=pl.DeviceIdType.MESH)

    greet({"vert": near})
    greet({"vert": far})
    pl.when(has_below)(lambda: greet({"gz": slab - 1}))
    pl.when(has_above)(lambda: greet({"gz": slab + 1}))
    pl.semaphore_wait(barrier, 2 + jnp.minimum(slab, 1) + jnp.minimum(slabs - 1 - slab, 1))

    chunks = [
        pl.ds(0, radius),
        pl.ds(planes + radius, radius),
        pl.ds(radius, half),
        pl.ds(radius + half, half),
    ]
    waits = []
    stage_a = []
    for chunk in chunks:
        passing = remote(partial.at[rows(near_far), chunk], got_a.at[1, :, chunk], {"vert": near})
        passing.start()
        staying = remote(partial.at[rows(near), chunk], got_a.at[0, :, chunk], {"vert": near})
        staying.start()
        stage_a.append((passing, staying))
        waits += [passing, staying]

    @pl.when(jnp.logical_not(has_below))
    def _():
        got_halo[0] = jnp.zeros(got_halo.shape[1:], got_halo.dtype)

    @pl.when(jnp.logical_not(has_above))
    def _():
        got_halo[1] = jnp.zeros(got_halo.shape[1:], got_halo.dtype)

    if not last:

        @pl.when(jnp.logical_not(has_below))
        def _():
            result[pl.ds(0, radius), rows(part)] = jnp.zeros(
                (radius, rows_q, result.shape[2]), result.dtype
            )

        @pl.when(jnp.logical_not(has_above))
        def _():
            result[pl.ds(planes + radius, radius), rows(part)] = jnp.zeros(
                (radius, rows_q, result.shape[2]), result.dtype
            )

    stage_b = []
    for chunk, (passing, _) in zip(chunks, stage_a):
        passing.wait_recv()
        forward[:, chunk] = partial[rows(far), chunk] + got_a[1, :, chunk]
        copy = remote(forward.at[:, chunk], got_b.at[:, chunk], {"vert": far})
        copy.start()
        stage_b.append(copy)
        waits.append(copy)

    def total(place):
        chunk = chunks[place]
        stage_a[place][1].wait_recv()
        stage_b[place].wait_recv()
        return (partial[rows(part), chunk] + got_a[0, :, chunk]) + got_b[:, chunk]

    edge[0] = total(0)
    down = remote(edge.at[0], got_halo.at[1], {"gz": slab - 1})
    pl.when(has_below)(lambda: down.start())
    edge[1] = total(1)
    up = remote(edge.at[1], got_halo.at[0], {"gz": slab + 1})
    pl.when(has_above)(lambda: up.start())

    inner = 0 if last else radius
    shared = []
    besides = []
    moved = []
    for place in range(2):
        summed = total(2 + place)
        if place == 0:
            pl.when(has_below)(lambda: up.wait_recv())
        else:
            pl.when(has_above)(lambda: down.wait_recv())
        own = pl.ds(place * half, half)
        value = held[own] * jnp.swapaxes(summed + got_halo[place], 0, 1) / VIEWS
        if not last:
            renewed[own] = value
        target = result.at[pl.ds(inner + place * half, half), rows(part)]
        target[...] = value.astype(result.dtype)
        if not last:
            if place == 0:
                copy = remote(
                    target, result.at[pl.ds(planes + radius, radius), rows(part)], {"gz": slab - 1}
                )
                pl.when(has_below)(functools.partial(copy.start))
            else:
                copy = remote(target, result.at[pl.ds(0, radius), rows(part)], {"gz": slab + 1})
                pl.when(has_above)(functools.partial(copy.start))
            moved.append(copy)
        across = remote(target, target, {"vert": far})
        across.start()
        beside = remote(target, target, {"vert": near})
        beside.start()
        shared.append((inner + place * half, half, across))
        waits += [across, beside]
        besides.append(beside)
    late = []

    def relay(start, length, across):
        across.wait_recv()
        target = result.at[pl.ds(start, length), rows(far)]
        copy = remote(target, target, {"vert": near})
        copy.start()
        late.append(copy)

    if last:
        for item in shared:
            relay(*item)
    else:
        relay(*shared[0])
        relay(*shared[1])
        outer = []
        for place in range(2):
            start = planes + radius if place == 0 else 0
            pl.when(has_above if place == 0 else has_below)(
                functools.partial(moved[place].wait_recv)
            )
            target = result.at[pl.ds(start, radius), rows(part)]
            across = remote(target, target, {"vert": far})
            across.start()
            beside = remote(target, target, {"vert": near})
            beside.start()
            outer.append((start, radius, across))
            late.append(beside)
        for item in outer:
            relay(*item)
            waits.append(item[2])
        pl.when(has_below)(lambda: moved[0].wait_send())
        pl.when(has_above)(lambda: moved[1].wait_send())
    pl.when(has_below)(lambda: down.wait_send())
    pl.when(has_above)(lambda: up.wait_send())
    for copy in waits:
        copy.wait_send()
    for copy in late:
        copy.wait_send()
        copy.wait_recv()
    for copy in besides:
        copy.wait_recv()


def exchange(partial, held, last):
    rows_x, whole, rows_y = partial.shape
    planes, rows_q, _ = held.shape
    radius = (whole - planes) // 2
    assert planes == 2 * radius and rows_x == 4 * rows_q
    vmem = pl.BlockSpec(memory_space=pltpu.VMEM)
    f32 = jnp.float32
    if last:
        out_shape = jax.ShapeDtypeStruct((planes, rows_x, rows_y), f32)
        out_specs = vmem
    else:
        out_shape = (
            jax.ShapeDtypeStruct(held.shape, f32),
            jax.ShapeDtypeStruct((whole, rows_x, rows_y), jnp.bfloat16),
        )
        out_specs = (vmem, vmem)
    copies = 20 if last else 28
    return pl.pallas_call(
        functools.partial(exchange_kernel, last),
        out_shape=out_shape,
        in_specs=[vmem, vmem],
        out_specs=out_specs,
        scratch_shapes=[
            pltpu.VMEM((2, rows_q, whole, rows_y), f32),
            pltpu.VMEM((rows_q, whole, rows_y), f32),
            pltpu.VMEM((rows_q, whole, rows_y), f32),
            pltpu.VMEM((2, rows_q, radius, rows_y), f32),
            pltpu.VMEM((2, rows_q, radius, rows_y), f32),
            pltpu.SemaphoreType.DMA((copies,)),
            pltpu.SemaphoreType.DMA((copies,)),
        ],
        compiler_params=pltpu.CompilerParams(
            collective_id=1 if last else 0, has_side_effects=True, vmem_limit_bytes=VMEM_LIMIT
        ),
        name="finish" if last else "renew",
    )(partial, held)


def body(estimate, raw_views, block_dest, lateral_psf, axial_psf):
    planes, rows_x, rows_y = estimate.shape
    along_x = normalize(lateral_psf[:, 0])
    along_y = normalize(lateral_psf[:, 1])
    depth = normalize(axial_psf)
    radius = (axial_psf.shape[1] - 1) // 2
    mat_x = band_matrix(along_x, rows_x)
    mat_y = band_matrix(along_y, rows_y)
    front_matrix = axial_matrix(depth, planes)
    parts = lax.axis_size("vert")
    rows_q = rows_x // parts
    mine = lax.axis_index("vert") * rows_q
    held = lax.dynamic_slice_in_dim(estimate, mine, rows_q, axis=1)
    slabs = lax.axis_size("gz")
    packed, extra = pack(source_of(block_dest), raw_views, slabs, block_dest.shape[1] // slabs)
    widened, main, late, dests = spread(estimate, packed, extra, block_dest, radius)
    observed = place(origin_of(dests), main, late).reshape(-1, planes, rows_x, rows_y)
    for iteration in range(ITERS):
        first = jnp.einsum(
            "vzp,pxy->vzxy", front_matrix, widened, preferred_element_type=jnp.float32
        ).astype(jnp.bfloat16)
        second = jnp.einsum(
            "vik,vzky->vziy", mat_x, first, preferred_element_type=jnp.float32
        ).astype(jnp.bfloat16)
        blurred = jnp.einsum("vzxl,vjl->vzxj", second, mat_y, preferred_element_type=jnp.float32)
        ratio = (observed.astype(jnp.float32) / blurred).astype(jnp.bfloat16)
        third = jnp.einsum(
            "vzxj,vjl->vzxl", ratio, mat_y, preferred_element_type=jnp.float32
        ).astype(jnp.bfloat16)
        fourth = jnp.einsum(
            "vik,vziy->vzky", mat_x, third, preferred_element_type=jnp.float32
        ).astype(jnp.bfloat16)
        partial_back = jnp.einsum(
            "vzp,vzxy->xpy", front_matrix, fourth, preferred_element_type=jnp.float32
        )
        if iteration < ITERS - 1:
            held, widened = exchange(partial_back, held, False)
        else:
            held = exchange(partial_back, held, True)
    return held


def solution(mesh):
    return jax.shard_map(
        body,
        mesh=mesh,
        in_specs=(
            P("gz", None, None),
            P("vert", "gz", None, None),
            P("vert", "gz"),
            P("vert", None, None),
            P("vert", None),
        ),
        out_specs=P("gz", None, None),
        check_vma=False,
    )
```
